32 devices in a mesh: groups: 2 (over x), col: 16 (over z, y, core).
Axes of the slice: x: 2, y: 2, z: 4, core: 2. Of those that a mesh axis runs over, the one named last changes fastest.
Arguments:
- pupils: bfloat16 [2, 32, 6144], P(None, ('groups', 'col')), parts along dimension 1, may hold values from -6 to 6
- phase_tangent: float32 [6144], replicated, may hold values from -6 to 6
- weights: float32 [32], P(('groups', 'col')), parts along dimension 0, may hold values from 0.01 to 0.1
- weight_tangent: float32 [32], P(('groups', 'col')), parts along dimension 0, may hold values from -0.3 to 0.3
- offsets: int32 [32], P(('groups', 'col')), parts along dimension 0, may hold values from 0 to 1023
- row_support: int32 [4096], P('groups'), parts along dimension 0, may hold values from 0 to 5119, as said below
- col_support: int32 [4096], replicated, may hold values from 0 to 5119, as said below
Outputs:
- tcc_tangent: float32 [2, 4096, 4096], P(None, 'groups', 'col'), parts along dimension 1
The draws below stay inside these ranges and needn't reach their ends.
There are 2 independent parts, one for each index of `groups`. The reference program is written for one: setup_inputs(seed, part) draws one part's arguments, and reference() takes and returns one part's arrays. A program takes and returns all parts, laid end to end along the dimension named above; an argument that names none is the same for every part. Nothing has to cross between parts.
Inputs may be any that keep to these rules, and one draw needn't show every extreme that they name: `row_support`: distinct grid positions. `col_support`: distinct grid positions.
All inputs are finite; a program needn't handle non-finite values.
Results may differ from the reference program's by a relative error of at most 0.0034.
Values may be sent and summed in bfloat16 or wider, within the bound.
A program may use at most 128 MiB of HBM per device.

```python
import math
import jax
import jax.numpy as jnp
from jax import lax

R = 2048
NF = 4096
S = 16
GRID = 6144
SHIFT = 1024


def draw_offsets(key, part):
    key = jax.random.fold_in(key, 11)
    values = jax.random.randint(key, (S,), 0, SHIFT, dtype=jnp.int32)
    values = values.at[0].set(SHIFT - 1)
    values = values.at[1].set(0)
    return values.astype(jnp.int32)


def support_positions(key, count):
    top = GRID - SHIFT - 1
    inner = jax.random.permutation(jax.random.fold_in(key, 1), top - 1)[:count - 2].astype(jnp.int32) + 1
    ends = jnp.array([0, top], dtype=jnp.int32)
    joined = jnp.concatenate([inner, ends])
    turn = jax.random.randint(jax.random.fold_in(key, 2), (), 0, count, dtype=jnp.int32)
    return jnp.roll(joined, turn).astype(jnp.int32)


def draw_row_support(key, part):
    key = jax.random.fold_in(key, 12)
    return support_positions(key, R)


def draw_col_support(key, part):
    key = jax.random.fold_in(key, 13)
    return support_positions(key, NF)


def shard_levels(rng, extent, pieces, smallest, top_value):
    factor_of = 1.0
    for axis_at, shards_of in pieces:
        steps = jax.random.uniform(jax.random.fold_in(jax.random.fold_in(rng, 6), axis_at), (shards_of,), jnp.float32, smallest / len(pieces), top_value / len(pieces))
        factor_of = factor_of * jnp.repeat(jnp.exp(steps), extent[axis_at] // shards_of).reshape((-1,) + (1,) * (len(extent) - 1 - axis_at))
    return factor_of


def gaussian(rng, extent, scale, bound, split=(), kind=jnp.bfloat16):
    result = jax.random.normal(rng, extent, jnp.float32) * scale
    if len(split) > 0:
        result = shard_levels(rng, extent, split, -0.22, 0.18) * result
    return jnp.clip(result, min=-bound, max=bound).astype(kind)


def setup_inputs(seed: int = 0, part: int = 0) -> dict:
    arg_keys = jax.random.split(jax.random.key(seed), 8)
    part_splits = jax.random.split(jax.random.fold_in(arg_keys[7], part), 8)
    return {
        "pupils": gaussian(part_splits[0], (2, S, GRID), 1.0, 6.0, ((1, 16),)),
        "phase_tangent": gaussian(arg_keys[1], (GRID,), 1.0, 6.0, (), jnp.float32),
        "weights": jnp.clip(jnp.exp(math.log(0.1) - 2.3025851 * jax.random.uniform(part_splits[2], (S,), jnp.float32) ** shard_levels(part_splits[2], (S,), ((0, 16),), -0.2, 0.2)), 0.01, 0.1),
        "weight_tangent": gaussian(part_splits[3], (S,), 0.05, 0.3, ((0, 16),), jnp.float32),
        "offsets": draw_offsets(jax.random.fold_in(jax.random.fold_in(arg_keys[7], part), 71), part),
        "row_support": draw_row_support(jax.random.fold_in(jax.random.fold_in(arg_keys[7], part), 71), part),
        "col_support": draw_col_support(jax.random.fold_in(arg_keys[7], 71), part),
    }


def shifted_values(pupils, offsets, support, phase_tangent):
    shifted = (support[None, :] + offsets[:, None]).astype(jnp.int32)
    real_part = jnp.take_along_axis(pupils[0], shifted, axis=1)
    imag_part = jnp.take_along_axis(pupils[1], shifted, axis=1)
    slopes = phase_tangent[shifted]
    return real_part, imag_part, slopes


def source_product(left_side, right_side):
    return lax.dot_general(left_side, right_side, (((0,), (0,)), ((), ())), precision=lax.Precision.HIGHEST, preferred_element_type=jnp.float32)


def reference(pupils, phase_tangent, weights, weight_tangent, offsets, row_support, col_support):
    row_real, row_imag, row_slopes = shifted_values(pupils, offsets, row_support, phase_tangent)
    d_real = (-row_slopes * row_imag.astype(jnp.float32)).astype(jnp.bfloat16)
    d_imag = (row_slopes * row_real.astype(jnp.float32)).astype(jnp.bfloat16)
    col_real, col_imag, col_slopes = shifted_values(pupils, offsets, col_support, phase_tangent)
    real_f = col_real.astype(jnp.float32)
    imag_f = col_imag.astype(jnp.float32)
    tangent_col = weight_tangent[:, None]
    weight_col = weights[:, None]
    x_real = (tangent_col * real_f - weight_col * col_slopes * imag_f).astype(jnp.bfloat16)
    x_imag = (tangent_col * imag_f + weight_col * col_slopes * real_f).astype(jnp.bfloat16)
    y_real = (weight_col * real_f).astype(jnp.bfloat16)
    y_imag = (weight_col * imag_f).astype(jnp.bfloat16)
    left_real = jnp.concatenate([row_real, d_real], axis=0).astype(jnp.float32)
    left_imag = jnp.concatenate([row_imag, d_imag], axis=0).astype(jnp.float32)
    right_real = jnp.concatenate([x_real, y_real], axis=0).astype(jnp.float32)
    right_imag = jnp.concatenate([x_imag, y_imag], axis=0).astype(jnp.float32)
    real_sum = source_product(left_real, right_real) + source_product(left_imag, right_imag)
    imag_sum = source_product(left_real, right_imag) - source_product(left_imag, right_real)
    return jnp.stack([real_sum, imag_sum])
```

```python
import functools

import jax
import jax.numpy as jnp
from jax import lax
from jax.experimental import pallas as pl
from jax.experimental.pallas import tpu as pltpu
from jax.sharding import PartitionSpec as P

LANES = 128
SCALAR_ROWS = 16
PARTS = 8
TABLE_LIMIT_BYTES = 8 * 1024 * 1024
MESH = pl.DeviceIdType.MESH


def shifted_values(pupils, offsets, support, phase_tangent):
    shifted = support[None, :] + offsets[:, None]
    real_part = jnp.take_along_axis(pupils[0], shifted, axis=1)
    imag_part = jnp.take_along_axis(pupils[1], shifted, axis=1)
    slopes = phase_tangent[shifted]
    return (real_part, imag_part, slopes)


def column_factors(real_part, imag_part, slopes, weights, weight_tangent):
    real_f = real_part.astype(jnp.float32)
    imag_f = imag_part.astype(jnp.float32)
    tangent_col = weight_tangent[:, None]
    weight_col = weights[:, None]
    x_real = (tangent_col * real_f - weight_col * slopes * imag_f).astype(jnp.bfloat16)
    x_imag = (tangent_col * imag_f + weight_col * slopes * real_f).astype(jnp.bfloat16)
    y_real = (weight_col * real_f).astype(jnp.bfloat16)
    y_imag = (weight_col * imag_f).astype(jnp.bfloat16)
    return jnp.stack([jnp.stack([x_real, y_real]), jnp.stack([x_imag, y_imag])])


def block_product(left_rows, col_block):
    width = col_block.shape[3]
    depth = 4 * col_block.shape[2]
    left_all = left_rows.reshape(depth, left_rows.shape[3])
    right_for_real = jnp.concatenate([col_block[0], col_block[1]], axis=0)
    right_for_imag = jnp.concatenate([col_block[1], -col_block[0]], axis=0)
    right_all = jnp.concatenate([right_for_real, right_for_imag], axis=2).reshape(depth, 2 * width)
    product = lax.dot_general(
        left_all, right_all, (((0,), (0,)), ((), ())), preferred_element_type=jnp.float32
    )
    return jnp.stack([product[:, :width], product[:, width:]])


def exchanged(pupils, phase_tangent, weights, weight_tangent, offsets, row_support, col_support):
    col_real, col_imag, col_slopes = shifted_values(pupils, offsets, col_support, phase_tangent)
    columns = column_factors(col_real, col_imag, col_slopes, weights, weight_tangent)
    col_block = lax.all_to_all(columns, "col", split_axis=3, concat_axis=2, tiled=True)
    row_real, row_imag, row_slopes = shifted_values(pupils, offsets, row_support, phase_tangent)
    d_real = (-row_slopes * row_imag.astype(jnp.float32)).astype(jnp.bfloat16)
    d_imag = (row_slopes * row_real.astype(jnp.float32)).astype(jnp.bfloat16)
    rows = jnp.stack([jnp.stack([row_real, d_real]), jnp.stack([row_imag, d_imag])])
    left_rows = lax.all_gather(rows, "col", axis=2, tiled=True)
    return block_product(left_rows, col_block)


def split3(value):
    high = value.astype(jnp.bfloat16).astype(jnp.float32)
    rest = value - high
    middle = rest.astype(jnp.bfloat16).astype(jnp.float32)
    return high, middle, rest - middle


def gather_kernel(n, chunks, pupil_ref, w_ref, wt_ref, off_ref, out_ref, wide, packed, send_sem, recv_sem, own_sem):
    me = lax.axis_index("col")
    barrier = pltpu.get_barrier_semaphore()
    for k in range(1, n):
        pl.semaphore_signal(barrier, inc=1, device_id={"col": lax.rem(me + k, n)}, device_id_type=MESH)

    values = pupil_ref[...].astype(jnp.float32)
    for part in range(2):
        for chunk in range(chunks):
            row = part * chunks + chunk
            wide[row : row + 1, :] = values[part : part + 1, chunk * LANES : (chunk + 1) * LANES]
    lane = lax.broadcasted_iota(jnp.int32, (SCALAR_ROWS, LANES), 1)
    scalars = jnp.zeros((SCALAR_ROWS, LANES), jnp.float32)
    place = 0
    for scalar in (w_ref[0], wt_ref[0], off_ref[0].astype(jnp.float32)):
        for piece in split3(jnp.full((SCALAR_ROWS, LANES), scalar, jnp.float32)):
            scalars = jnp.where(lane == place, piece, scalars)
            place += 1
    wide[2 * chunks :, :] = scalars
    packed[...] = wide[...].astype(jnp.bfloat16)

    own = pltpu.make_async_copy(packed, out_ref.at[me], own_sem)
    own.start()
    pl.semaphore_wait(barrier, n - 1)
    copies = []
    for k in range(1, n):
        copy = pltpu.make_async_remote_copy(
            src_ref=packed,
            dst_ref=out_ref.at[me],
            send_sem=send_sem.at[k - 1],
            recv_sem=recv_sem.at[k - 1],
            device_id={"col": lax.rem(me + k, n)},
            device_id_type=MESH,
        )
        copy.start()
        copies.append(copy)
    own.wait()
    for copy in copies:
        copy.wait()


def gathered_pupils(n, pupils, weights, weight_tangent, offsets):
    grid_size = pupils.shape[2]
    chunks = grid_size // LANES
    rows = 2 * chunks + SCALAR_ROWS
    smem = pl.BlockSpec(memory_space=pltpu.SMEM)
    return pl.pallas_call(
        functools.partial(gather_kernel, n, chunks),
        out_shape=jax.ShapeDtypeStruct((n, rows, LANES), jnp.bfloat16),
        in_specs=[pl.BlockSpec(memory_space=pltpu.VMEM), smem, smem, smem],
        out_specs=pl.BlockSpec(memory_space=pl.ANY),
        scratch_shapes=[
            pltpu.VMEM((rows, LANES), jnp.float32),
            pltpu.VMEM((rows, LANES), jnp.bfloat16),
            pltpu.SemaphoreType.DMA((n - 1,)),
            pltpu.SemaphoreType.DMA((n - 1,)),
            pltpu.SemaphoreType.DMA,
        ],
        compiler_params=pltpu.CompilerParams(collective_id=0, has_side_effects=True),
        name="gather_pupils",
    )(pupils.reshape(2, grid_size), weights, weight_tangent, offsets)


def rounded(value):
    return value.astype(jnp.bfloat16).astype(jnp.float32)


def shift_rows(source, start, reach, lane_shift, lane):
    lower = source[pl.ds(start, reach), :]
    upper = source[pl.ds(start + 1, reach), :]
    return pltpu.roll(jnp.where(lane >= lane_shift, lower, upper), lax.rem(LANES - lane_shift, LANES), 1)


def block_kernel(
    sources, chunks, reach, tile, width,
    offset_ref, row_ref, col_ref, all_ref, phase_ref, out_ref,
    wide, shifted, factors, table, picked, right,
):
    depth = 4 * sources

    def pick(index_ref, base, count):
        def eight(group, carry):
            first = pl.multiple_of(group * 8, 8)
            for k in range(8):
                picked[pl.ds(first + k, 1), :] = table[pl.ds(index_ref[base + first + k], 1), :]
            return carry

        lax.fori_loop(0, count // 8, eight, 0, unroll=4)

    @pl.when(pl.program_id(0) == 0)
    def _():
        lane = lax.broadcasted_iota(jnp.int32, (reach, LANES), 1)
        for s in range(sources):
            wide[...] = all_ref[s, : 2 * chunks, :].astype(jnp.float32)
            scalars = all_ref[s, 2 * chunks : 2 * chunks + SCALAR_ROWS, :].astype(jnp.float32)[:1, :]
            factors[s : s + 1, :] = jnp.broadcast_to(
                scalars[:, 0:1] + scalars[:, 1:2] + scalars[:, 2:3], (1, LANES)
            )
            factors[sources + s : sources + s + 1, :] = jnp.broadcast_to(
                scalars[:, 3:4] + scalars[:, 4:5] + scalars[:, 5:6], (1, LANES)
            )
            offset = offset_ref[s]
            start = offset // LANES
            lane_shift = lax.rem(offset, LANES)
            spread = pl.ds(s, reach, stride=sources)
            shifted[0, spread, :] = shift_rows(wide, start, reach, lane_shift, lane)
            shifted[1, spread, :] = shift_rows(wide, chunks + start, reach, lane_shift, lane)
            shifted[2, spread, :] = shift_rows(phase_ref, start, reach, lane_shift, lane)
        weight = factors[:sources, :]
        tangent = factors[sources:, :]

        def one_chunk(chunk, carry):
            at = pl.ds(pl.multiple_of(chunk * sources, sources), sources)
            real, imag, slope = shifted[0, at, :], shifted[1, at, :], shifted[2, at, :]
            tilted = weight * slope
            block = jnp.concatenate(
                [
                    real,
                    -slope * imag,
                    imag,
                    slope * real,
                    tangent * real - tilted * imag,
                    weight * real,
                    tangent * imag + tilted * real,
                    weight * imag,
                ],
                axis=0,
            )
            table[pl.ds(pl.multiple_of(chunk * LANES, LANES), LANES), :] = rounded(block).T
            return carry

        lax.fori_loop(0, reach, one_chunk, 0, unroll=2)

        pick(col_ref, 0, width)
        columns = pltpu.roll(picked[:width, :], PARTS * sources - depth, 1)
        column_lane = lax.broadcasted_iota(jnp.int32, (width, LANES), 1)
        swapped = pltpu.roll(columns, LANES - depth // 2, 1)
        crossed = pltpu.roll(columns, depth // 2, 1)
        zero = jnp.zeros_like(columns)
        right[:width, :] = jnp.where(column_lane < depth, columns, zero).astype(jnp.bfloat16)
        right[width:, :] = jnp.where(
            column_lane < depth // 2, swapped, jnp.where(column_lane < depth, -crossed, zero)
        ).astype(jnp.bfloat16)

    pick(row_ref, pl.program_id(0) * tile, tile)
    product = lax.dot_general(
        picked[:tile, :].astype(jnp.bfloat16), right[...], (((1,), (1,)), ((), ())),
        preferred_element_type=jnp.float32,
    )
    out_ref[0] = product[:, :width]
    out_ref[1] = product[:, width:]


def block_row(sources, reach, everything, offsets, phase_tangent, row_support, col_here):
    chunks = phase_tangent.shape[0] // LANES
    rows, width = row_support.shape[0], col_here.shape[0]
    tile = 256
    whole = pl.BlockSpec(memory_space=pltpu.VMEM)
    smem = pl.BlockSpec(memory_space=pltpu.SMEM)
    return pl.pallas_call(
        functools.partial(block_kernel, sources, chunks, reach, tile, width),
        out_shape=jax.ShapeDtypeStruct((2, rows, width), jnp.float32),
        grid=(rows // tile,),
        in_specs=[smem, smem, smem, whole, whole],
        out_specs=pl.BlockSpec((2, tile, width), lambda i: (0, i, 0)),
        scratch_shapes=[
            pltpu.VMEM((2 * chunks, LANES), jnp.float32),
            pltpu.VMEM((3, reach * sources, LANES), jnp.float32),
            pltpu.VMEM((2 * sources, LANES), jnp.float32),
            pltpu.VMEM((reach * LANES, LANES), jnp.float32),
            pltpu.VMEM((max(tile, width), LANES), jnp.float32),
            pltpu.VMEM((2 * width, LANES), jnp.bfloat16),
        ],
        compiler_params=pltpu.CompilerParams(vmem_limit_bytes=32 * 1024 * 1024),
        name="block_row",
    )(offsets, row_support, col_here, everything, phase_tangent.reshape(chunks, LANES))


def local(n, pupils, phase_tangent, weights, weight_tangent, offsets, row_support, col_support):
    grid_size = phase_tangent.shape[0]
    rows = row_support.shape[0]
    width = col_support.shape[0] // n
    reach = grid_size // 6 * 5 // LANES
    fits = (
        PARTS * n == LANES
        and grid_size % (6 * LANES) == 0
        and rows % 256 == 0
        and width % LANES == 0
        and grid_size * LANES * 4 <= TABLE_LIMIT_BYTES
    )
    if not fits:
        return exchanged(pupils, phase_tangent, weights, weight_tangent, offsets, row_support, col_support)
    everything = gathered_pupils(n, pupils, weights, weight_tangent, offsets)
    start = 2 * (grid_size // LANES)
    all_offsets = everything[:, start, 6:9].astype(jnp.float32).sum(axis=1).astype(jnp.int32)
    col_here = lax.dynamic_slice(col_support, (lax.axis_index("col") * width,), (width,))
    return block_row(n, reach, everything, all_offsets, phase_tangent, row_support, col_here)


def solution(mesh):
    in_specs = (
        P(None, ("groups", "col"), None),
        P(),
        P(("groups", "col")),
        P(("groups", "col")),
        P(("groups", "col")),
        P("groups"),
        P(),
    )
    out_specs = P(None, "groups", "col")
    return jax.shard_map(
        functools.partial(local, mesh.shape["col"]),
        mesh=mesh, in_specs=in_specs, out_specs=out_specs, check_vma=False,
    )
```

```python
import functools

import jax
import jax.numpy as jnp
from jax import lax
from jax.experimental import pallas as pl
from jax.experimental.pallas import tpu as pltpu
from jax.sharding import PartitionSpec as P

LANES = 128
SCALAR_ROWS = 16
PARTS = 8
PICKS = 32
TABLE_LIMIT_BYTES = 8 * 1024 * 1024
MESH = pl.DeviceIdType.MESH


def shifted_values(pupils, offsets, support, phase_tangent):
    shifted = support[None, :] + offsets[:, None]
    real_part = jnp.take_along_axis(pupils[0], shifted, axis=1)
    imag_part = jnp.take_along_axis(pupils[1], shifted, axis=1)
    slopes = phase_tangent[shifted]
    return (real_part, imag_part, slopes)


def column_factors(real_part, imag_part, slopes, weights, weight_tangent):
    real_f = real_part.astype(jnp.float32)
    imag_f = imag_part.astype(jnp.float32)
    tangent_col = weight_tangent[:, None]
    weight_col = weights[:, None]
    x_real = (tangent_col * real_f - weight_col * slopes * imag_f).astype(jnp.bfloat16)
    x_imag = (tangent_col * imag_f + weight_col * slopes * real_f).astype(jnp.bfloat16)
    y_real = (weight_col * real_f).astype(jnp.bfloat16)
    y_imag = (weight_col * imag_f).astype(jnp.bfloat16)
    return jnp.stack([jnp.stack([x_real, y_real]), jnp.stack([x_imag, y_imag])])


def block_product(left_rows, col_block):
    width = col_block.shape[3]
    depth = 4 * col_block.shape[2]
    left_all = left_rows.reshape(depth, left_rows.shape[3])
    right_for_real = jnp.concatenate([col_block[0], col_block[1]], axis=0)
    right_for_imag = jnp.concatenate([col_block[1], -col_block[0]], axis=0)
    right_all = jnp.concatenate([right_for_real, right_for_imag], axis=2).reshape(depth, 2 * width)
    product = lax.dot_general(
        left_all, right_all, (((0,), (0,)), ((), ())), preferred_element_type=jnp.float32
    )
    return jnp.stack([product[:, :width], product[:, width:]])


def exchanged(pupils, phase_tangent, weights, weight_tangent, offsets, row_support, col_support):
    col_real, col_imag, col_slopes = shifted_values(pupils, offsets, col_support, phase_tangent)
    columns = column_factors(col_real, col_imag, col_slopes, weights, weight_tangent)
    col_block = lax.all_to_all(columns, "col", split_axis=3, concat_axis=2, tiled=True)
    row_real, row_imag, row_slopes = shifted_values(pupils, offsets, row_support, phase_tangent)
    d_real = (-row_slopes * row_imag.astype(jnp.float32)).astype(jnp.bfloat16)
    d_imag = (row_slopes * row_real.astype(jnp.float32)).astype(jnp.bfloat16)
    rows = jnp.stack([jnp.stack([row_real, d_real]), jnp.stack([row_imag, d_imag])])
    left_rows = lax.all_gather(rows, "col", axis=2, tiled=True)
    return block_product(left_rows, col_block)


def split3(value):
    high = value.astype(jnp.bfloat16).astype(jnp.float32)
    rest = value - high
    middle = rest.astype(jnp.bfloat16).astype(jnp.float32)
    return high, middle, rest - middle


def gather_kernel(
    n, chunks, pupil_hbm, w_ref, wt_ref, off_ref, out_ref, pupil_ref, wide, packed, send_sem, recv_sem, own_sem
):
    load = pltpu.make_async_copy(pupil_hbm, pupil_ref, own_sem)
    load.start()
    me = lax.axis_index("col")
    quarter = n // 4
    core = lax.rem(me, 2)
    far = quarter * (me // quarter)
    near = lax.rem(me, quarter)
    sibling = far + near + 1 - 2 * core
    across_near = lax.rem(near + quarter // 2, quarter)
    across = far + across_near

    def ahead(k):
        return lax.rem(me + k * quarter, n)

    barrier = pltpu.get_barrier_semaphore()
    partners = [ahead(1), ahead(2), ahead(3), across, sibling]
    for partner in partners:
        pl.semaphore_signal(barrier, inc=1, device_id={"col": partner}, device_id_type=MESH)

    load.wait()
    values = pupil_ref[...].astype(jnp.float32)
    for part in range(2):
        for chunk in range(chunks):
            row = part * chunks + chunk
            wide[row : row + 1, :] = values[part : part + 1, chunk * LANES : (chunk + 1) * LANES]
    lane = lax.broadcasted_iota(jnp.int32, (SCALAR_ROWS, LANES), 1)
    scalars = jnp.zeros((SCALAR_ROWS, LANES), jnp.float32)
    place = 0
    for scalar in (w_ref[0], wt_ref[0], off_ref[0].astype(jnp.float32)):
        for piece in split3(jnp.full((SCALAR_ROWS, LANES), scalar, jnp.float32)):
            scalars = jnp.where(lane == place, piece, scalars)
            place += 1
    wide[2 * chunks :, :] = scalars
    packed[...] = wide[...].astype(jnp.bfloat16)

    own = pltpu.make_async_copy(packed, out_ref.at[me], own_sem)
    own.start()
    pl.semaphore_wait(barrier, len(partners))

    def send(source, slot, index, partner):
        copy = pltpu.make_async_remote_copy(
            src_ref=source,
            dst_ref=out_ref.at[slot],
            send_sem=send_sem.at[index],
            recv_sem=recv_sem.at[index],
            device_id={"col": partner},
            device_id_type=MESH,
        )
        copy.start()
        return copy

    copies = {k: send(packed, me, k, ahead(k)) for k in (2, 1, 3)}
    copies[4] = send(packed, me, 4, across)
    copies[8] = send(packed, me, 8, sibling)
    for k in (1, 3, 2):
        copies[k].wait_recv()
        slot = lax.rem(me + (4 - k) * quarter, n)
        copies[4 + k] = send(out_ref.at[slot], slot, 4 + k, across)
        copies[8 + k] = send(out_ref.at[slot], slot, 8 + k, sibling)
    for k in (0, 1, 3, 2):
        copies[4 + k].wait_recv()
        slot = lax.rem(far + (4 - k) * quarter, n) + across_near
        copies[12 + k] = send(out_ref.at[slot], slot, 12 + k, sibling)
    own.wait()
    for k in range(8):
        copies[8 + k].wait_recv()
    for k in range(1, 16):
        copies[k].wait_send()


def gathered_pupils(n, pupils, weights, weight_tangent, offsets):
    grid_size = pupils.shape[2]
    chunks = grid_size // LANES
    rows = 2 * chunks + SCALAR_ROWS
    smem = pl.BlockSpec(memory_space=pltpu.SMEM)
    return pl.pallas_call(
        functools.partial(gather_kernel, n, chunks),
        out_shape=jax.ShapeDtypeStruct((n, rows, LANES), jnp.bfloat16),
        in_specs=[pl.BlockSpec(memory_space=pltpu.HBM), smem, smem, smem],
        out_specs=pl.BlockSpec(memory_space=pltpu.HBM),
        scratch_shapes=[
            pltpu.VMEM((2, grid_size), jnp.bfloat16),
            pltpu.VMEM((rows, LANES), jnp.float32),
            pltpu.VMEM((rows, LANES), jnp.bfloat16),
            pltpu.SemaphoreType.DMA((16,)),
            pltpu.SemaphoreType.DMA((16,)),
            pltpu.SemaphoreType.DMA,
        ],
        compiler_params=pltpu.CompilerParams(collective_id=0, has_side_effects=True),
        name="gather_pupils",
    )(pupils.reshape(2, grid_size), weights, weight_tangent, offsets)


def rounded(value):
    return value.astype(jnp.bfloat16).astype(jnp.float32)


def shift_rows(source, start, reach, lane_shift, lane):
    lower = source[pl.ds(start, reach), :]
    upper = source[pl.ds(start + 1, reach), :]
    return pltpu.roll(jnp.where(lane >= lane_shift, lower, upper), lax.rem(LANES - lane_shift, LANES), 1)


def block_kernel(
    sources, chunks, reach, tile, width,
    row_hbm, col_hbm, all_hbm, phase_hbm, out_ref,
    rows, cols, everything, phase, wide, shifted, factors, table, picked, right, sems,
):
    depth = 4 * sources

    def pick(index_ref, base, count):
        def some(group, carry):
            first = pl.multiple_of(group * PICKS, 8)
            for k in range(PICKS):
                picked[pl.ds(first + k, 1), :] = table[pl.ds(index_ref[base + first + k], 1), :]
            return carry

        lax.fori_loop(0, count // PICKS, some, 0)

    @pl.when(pl.program_id(0) == 0)
    def _():
        copies = [
            pltpu.make_async_copy(source, target, sems.at[i])
            for i, (source, target) in enumerate(
                [(all_hbm, everything), (phase_hbm, phase), (row_hbm, rows), (col_hbm, cols)]
            )
        ]
        for copy in copies:
            copy.start()
        copies[0].wait()
        copies[1].wait()
        lane = lax.broadcasted_iota(jnp.int32, (reach, LANES), 1)
        offsets = []
        for s in range(sources):
            scalars = everything[s, 2 * chunks : 2 * chunks + SCALAR_ROWS, :].astype(jnp.float32)[:1, :]
            one, two, three = (
                scalars[:, i : i + 1] + scalars[:, i + 1 : i + 2] + scalars[:, i + 2 : i + 3] for i in (0, 3, 6)
            )
            factors[s : s + 1, :] = jnp.broadcast_to(one, (1, LANES))
            factors[sources + s : sources + s + 1, :] = jnp.broadcast_to(two, (1, LANES))
            offsets.append(three[0, 0].astype(jnp.int32))
        for s in range(sources):
            own = wide.at[s % 2]
            own[...] = everything[s, : 2 * chunks, :].astype(jnp.float32)
            start = offsets[s] // LANES
            lane_shift = lax.rem(offsets[s], LANES)
            spread = pl.ds(s, reach, stride=sources)
            shifted[0, spread, :] = shift_rows(own, start, reach, lane_shift, lane)
            shifted[1, spread, :] = shift_rows(own, chunks + start, reach, lane_shift, lane)
            shifted[2, spread, :] = shift_rows(phase, start, reach, lane_shift, lane)
        weight = factors[:sources, :]
        tangent = factors[sources:, :]

        def one_chunk(chunk, carry):
            at = pl.ds(pl.multiple_of(chunk * sources, sources), sources)
            real, imag, slope = shifted[0, at, :], shifted[1, at, :], shifted[2, at, :]
            tilted = weight * slope
            block = jnp.concatenate(
                [
                    real,
                    -slope * imag,
                    imag,
                    slope * real,
                    tangent * real - tilted * imag,
                    weight * real,
                    tangent * imag + tilted * real,
                    weight * imag,
                ],
                axis=0,
            )
            table[pl.ds(pl.multiple_of(chunk * LANES, LANES), LANES), :] = rounded(block).T
            return carry

        lax.fori_loop(0, reach, one_chunk, 0, unroll=2)

        copies[2].wait()
        copies[3].wait()
        pick(cols, lax.axis_index("col") * width, width)
        columns = pltpu.roll(picked[:width, :], PARTS * sources - depth, 1)
        column_lane = lax.broadcasted_iota(jnp.int32, (width, LANES), 1)
        swapped = pltpu.roll(columns, LANES - depth // 2, 1)
        crossed = pltpu.roll(columns, depth // 2, 1)
        zero = jnp.zeros_like(columns)
        right[:width, :] = jnp.where(column_lane < depth, columns, zero).astype(jnp.bfloat16)
        right[width:, :] = jnp.where(
            column_lane < depth // 2, swapped, jnp.where(column_lane < depth, -crossed, zero)
        ).astype(jnp.bfloat16)

    pick(rows, pl.program_id(0) * tile, tile)
    product = lax.dot_general(
        picked[:tile, :].astype(jnp.bfloat16), right[...], (((1,), (1,)), ((), ())),
        preferred_element_type=jnp.float32,
    )
    out_ref[0] = product[:, :width]
    out_ref[1] = product[:, width:]


def block_row(sources, reach, everything, phase_tangent, row_support, col_support):
    chunks = phase_tangent.shape[0] // LANES
    rows, width = row_support.shape[0], col_support.shape[0] // sources
    tile = 256
    return pl.pallas_call(
        functools.partial(block_kernel, sources, chunks, reach, tile, width),
        out_shape=jax.ShapeDtypeStruct((2, rows, width), jnp.float32),
        grid=(rows // tile,),
        in_specs=[pl.BlockSpec(memory_space=pltpu.HBM)] * 4,
        out_specs=pl.BlockSpec((2, tile, width), lambda i: (0, i, 0)),
        scratch_shapes=[
            pltpu.SMEM(row_support.shape, jnp.int32),
            pltpu.SMEM(col_support.shape, jnp.int32),
            pltpu.VMEM(everything.shape, jnp.bfloat16),
            pltpu.VMEM((chunks, LANES), jnp.float32),
            pltpu.VMEM((2, 2 * chunks, LANES), jnp.float32),
            pltpu.VMEM((3, reach * sources, LANES), jnp.float32),
            pltpu.VMEM((2 * sources, LANES), jnp.float32),
            pltpu.VMEM((reach * LANES, LANES), jnp.float32),
            pltpu.VMEM((max(tile, width), LANES), jnp.float32),
            pltpu.VMEM((2 * width, LANES), jnp.bfloat16),
            pltpu.SemaphoreType.DMA((4,)),
        ],
        compiler_params=pltpu.CompilerParams(vmem_limit_bytes=48 * 1024 * 1024),
        name="block_row",
    )(row_support, col_support, everything, phase_tangent.reshape(chunks, LANES))


def local(n, pupils, phase_tangent, weights, weight_tangent, offsets, row_support, col_support):
    grid_size = phase_tangent.shape[0]
    rows = row_support.shape[0]
    width = col_support.shape[0] // n
    reach = grid_size // 6 * 5 // LANES
    fits = (
        PARTS * n == LANES
        and grid_size % (6 * LANES) == 0
        and rows % 256 == 0
        and width % LANES == 0
        and grid_size * LANES * 4 <= TABLE_LIMIT_BYTES
    )
    if not fits:
        return exchanged(pupils, phase_tangent, weights, weight_tangent, offsets, row_support, col_support)
    everything = gathered_pupils(n, pupils, weights, weight_tangent, offsets)
    return block_row(n, reach, everything, phase_tangent, row_support, col_support)


def solution(mesh):
    in_specs = (
        P(None, ("groups", "col"), None),
        P(),
        P(("groups", "col")),
        P(("groups", "col")),
        P(("groups", "col")),
        P("groups"),
        P(),
    )
    out_specs = P(None, "groups", "col")
    return jax.shard_map(
        functools.partial(local, mesh.shape["col"]),
        mesh=mesh, in_specs=in_specs, out_specs=out_specs, check_vma=False,
    )
```

```python
import functools

import jax
import jax.numpy as jnp
from jax import lax
from jax.experimental import pallas as pl
from jax.experimental.pallas import tpu as pltpu
from jax.sharding import PartitionSpec as P

LANES = 128
PARTS = 8
PICKS = 64
TILE = 512
ORDER = (1, 7, 2, 6, 3, 5, 4)
TABLE_LIMIT_BYTES = 8 * 1024 * 1024
MESH = pl.DeviceIdType.MESH


def shifted_values(pupils, offsets, support, phase_tangent):
    shifted = support[None, :] + offsets[:, None]
    real_part = jnp.take_along_axis(pupils[0], shifted, axis=1)
    imag_part = jnp.take_along_axis(pupils[1], shifted, axis=1)
    slopes = phase_tangent[shifted]
    return (real_part, imag_part, slopes)


def column_factors(real_part, imag_part, slopes, weights, weight_tangent):
    real_f = real_part.astype(jnp.float32)
    imag_f = imag_part.astype(jnp.float32)
    tangent_col = weight_tangent[:, None]
    weight_col = weights[:, None]
    x_real = (tangent_col * real_f - weight_col * slopes * imag_f).astype(jnp.bfloat16)
    x_imag = (tangent_col * imag_f + weight_col * slopes * real_f).astype(jnp.bfloat16)
    y_real = (weight_col * real_f).astype(jnp.bfloat16)
    y_imag = (weight_col * imag_f).astype(jnp.bfloat16)
    return jnp.stack([jnp.stack([x_real, y_real]), jnp.stack([x_imag, y_imag])])


def block_product(left_rows, col_block):
    width = col_block.shape[3]
    depth = 4 * col_block.shape[2]
    left_all = left_rows.reshape(depth, left_rows.shape[3])
    right_for_real = jnp.concatenate([col_block[0], col_block[1]], axis=0)
    right_for_imag = jnp.concatenate([col_block[1], -col_block[0]], axis=0)
    right_all = jnp.concatenate([right_for_real, right_for_imag], axis=2).reshape(depth, 2 * width)
    product = lax.dot_general(
        left_all, right_all, (((0,), (0,)), ((), ())), preferred_element_type=jnp.float32
    )
    return jnp.stack([product[:, :width], product[:, width:]])


def exchanged(pupils, phase_tangent, weights, weight_tangent, offsets, row_support, col_support):
    col_real, col_imag, col_slopes = shifted_values(pupils, offsets, col_support, phase_tangent)
    columns = column_factors(col_real, col_imag, col_slopes, weights, weight_tangent)
    col_block = lax.all_to_all(columns, "col", split_axis=3, concat_axis=2, tiled=True)
    row_real, row_imag, row_slopes = shifted_values(pupils, offsets, row_support, phase_tangent)
    d_real = (-row_slopes * row_imag.astype(jnp.float32)).astype(jnp.bfloat16)
    d_imag = (row_slopes * row_real.astype(jnp.float32)).astype(jnp.bfloat16)
    rows = jnp.stack([jnp.stack([row_real, d_real]), jnp.stack([row_imag, d_imag])])
    left_rows = lax.all_gather(rows, "col", axis=2, tiled=True)
    return block_product(left_rows, col_block)


def split3(value):
    high = value.astype(jnp.bfloat16).astype(jnp.float32)
    rest = value - high
    middle = rest.astype(jnp.bfloat16).astype(jnp.float32)
    return high, middle, rest - middle


def half_rows(reach):
    return (reach + 16) // 16 * 16


def shift_rows(source, start, reach, lane_shift, lane):
    lower = source[pl.ds(start, reach), :]
    upper = source[pl.ds(start + 1, reach), :]
    return pltpu.roll(jnp.where(lane >= lane_shift, lower, upper), (LANES - lane_shift) & (LANES - 1), 1)


def gather_kernel(
    n, chunks, reach, pupil_hbm, w_ref, wt_ref, off_ref, out_ref,
    pupil, wide, lined, packed, send_sem, recv_sem, own_sem,
):
    load = pltpu.make_async_copy(pupil_hbm, pupil, own_sem)
    load.start()
    me = lax.axis_index("col")
    sibling = me + 1 - 2 * lax.rem(me, 2)
    chips = n // 2

    def ahead(k):
        return lax.rem(me + 2 * k, n)

    barrier = pltpu.get_barrier_semaphore()
    for partner in [ahead(k) for k in range(1, chips)] + [sibling]:
        pl.semaphore_signal(barrier, inc=1, device_id={"col": partner}, device_id_type=MESH)

    half = half_rows(reach)
    scalar_rows = half - reach
    lane = lax.broadcasted_iota(jnp.int32, (scalar_rows, LANES), 1)
    scalars = jnp.zeros((scalar_rows, LANES), jnp.float32)
    place = 0
    for scalar in (w_ref[0], wt_ref[0], off_ref[0].astype(jnp.float32)):
        for piece in split3(jnp.full((scalar_rows, LANES), scalar, jnp.float32)):
            scalars = jnp.where(lane == place, piece, scalars)
            place += 1
    lined[reach:half, :] = scalars
    lined[half + reach :, :] = scalars
    start = lax.shift_right_logical(off_ref[0], LANES.bit_length() - 1)
    lane_shift = off_ref[0] & (LANES - 1)
    lane = lax.broadcasted_iota(jnp.int32, (reach, LANES), 1)
    load.wait()
    values = pupil[...].astype(jnp.float32)
    for part in range(2):
        for chunk in range(chunks):
            row = part * chunks + chunk
            wide[row : row + 1, :] = values[part : part + 1, chunk * LANES : (chunk + 1) * LANES]
    lined[:reach, :] = shift_rows(wide, start, reach, lane_shift, lane)
    lined[half : half + reach, :] = shift_rows(wide, chunks + start, reach, lane_shift, lane)
    packed[...] = lined[...].astype(jnp.bfloat16)

    own = pltpu.make_async_copy(packed, out_ref.at[me], own_sem)
    own.start()
    pl.semaphore_wait(barrier, chips)

    def send(source, slot, index, partner):
        copy = pltpu.make_async_remote_copy(
            src_ref=source,
            dst_ref=out_ref.at[slot],
            send_sem=send_sem.at[index],
            recv_sem=recv_sem.at[index],
            device_id={"col": partner},
            device_id_type=MESH,
        )
        copy.start()
        return copy

    copies = {k: send(packed, me, k, ahead(k)) for k in range(1, chips)}
    copies[chips] = send(packed, me, chips, sibling)
    for k in ORDER:
        copies[k].wait_recv()
        slot = ahead(chips - k)
        copies[chips + k] = send(out_ref.at[slot], slot, chips + k, sibling)
    own.wait()
    for k in range(chips):
        copies[chips + k].wait_recv()
    for k in range(1, n):
        copies[k].wait_send()


def gathered_pupils(n, reach, pupils, weights, weight_tangent, offsets):
    grid_size = pupils.shape[2]
    chunks = grid_size // LANES
    rows = 2 * half_rows(reach)
    smem = pl.BlockSpec(memory_space=pltpu.SMEM)
    return pl.pallas_call(
        functools.partial(gather_kernel, n, chunks, reach),
        out_shape=jax.ShapeDtypeStruct((n, rows, LANES), jnp.bfloat16),
        in_specs=[pl.BlockSpec(memory_space=pltpu.HBM), smem, smem, smem],
        out_specs=pl.BlockSpec(memory_space=pltpu.HBM),
        scratch_shapes=[
            pltpu.VMEM((2, grid_size), jnp.bfloat16),
            pltpu.VMEM((2 * chunks, LANES), jnp.float32),
            pltpu.VMEM((rows, LANES), jnp.float32),
            pltpu.VMEM((rows, LANES), jnp.bfloat16),
            pltpu.SemaphoreType.DMA((n,)),
            pltpu.SemaphoreType.DMA((n,)),
            pltpu.SemaphoreType.DMA,
        ],
        compiler_params=pltpu.CompilerParams(collective_id=0, has_side_effects=True),
        name="gather_pupils",
    )(pupils.reshape(2, grid_size), weights, weight_tangent, offsets)


def block_kernel(
    sources, chunks, reach, tile, width,
    row_hbm, col_hbm, all_hbm, phase_hbm, out_ref,
    rows, cols, everything, phase, shifted, factors, table, picked, right, sems,
):
    depth = 4 * sources

    def pick(index_ref, base, count):
        def some(group, carry):
            first = pl.multiple_of(group * PICKS, 8)
            for k in range(PICKS):
                picked[pl.ds(first + k, 1), :] = table[pl.ds(index_ref[base + first + k], 1), :]
            return carry

        lax.fori_loop(0, count // PICKS, some, 0)

    @pl.when(pl.program_id(0) == 0)
    def _():
        copies = [
            pltpu.make_async_copy(source, target, sems.at[i])
            for i, (source, target) in enumerate(
                [(all_hbm, everything), (phase_hbm, phase), (row_hbm, rows), (col_hbm, cols)]
            )
        ]
        for copy in copies:
            copy.start()
        copies[0].wait()
        copies[1].wait()
        lane = lax.broadcasted_iota(jnp.int32, (reach, LANES), 1)
        half = half_rows(reach)
        for s in range(sources):
            spread = pl.ds(s, reach, stride=sources)
            real = everything[s, :half, :].astype(jnp.float32)
            shifted[0, spread, :] = real[:reach, :]
            shifted[1, spread, :] = everything[s, half:, :].astype(jnp.float32)[:reach, :]
            scalars = real[reach : reach + 1, :]
            one, two, three = (
                scalars[:, i : i + 1] + scalars[:, i + 1 : i + 2] + scalars[:, i + 2 : i + 3] for i in (0, 3, 6)
            )
            factors[s : s + 1, :] = jnp.broadcast_to(one, (1, LANES))
            factors[sources + s : sources + s + 1, :] = jnp.broadcast_to(two, (1, LANES))
            offset = three[0, 0].astype(jnp.int32)
            start = lax.shift_right_logical(offset, LANES.bit_length() - 1)
            shifted[2, spread, :] = shift_rows(phase, start, reach, offset & (LANES - 1), lane)
        weight = factors[:sources, :]
        tangent = factors[sources:, :]

        def one_chunk(chunk, carry):
            at = pl.ds(pl.multiple_of(chunk * sources, sources), sources)
            real, imag, slope = shifted[0, at, :], shifted[1, at, :], shifted[2, at, :]
            tilted = weight * slope
            block = jnp.concatenate(
                [
                    real,
                    -slope * imag,
                    imag,
                    slope * real,
                    tangent * real - tilted * imag,
                    weight * real,
                    tangent * imag + tilted * real,
                    weight * imag,
                ],
                axis=0,
            )
            table[pl.ds(pl.multiple_of(chunk * LANES, LANES), LANES), :] = block.astype(jnp.bfloat16).T.astype(jnp.float32)
            return carry

        lax.fori_loop(0, reach, one_chunk, 0, unroll=8)

        copies[2].wait()
        copies[3].wait()
        pick(cols, lax.axis_index("col") * width, width)
        columns = pltpu.roll(picked[:width, :], PARTS * sources - depth, 1)
        column_lane = lax.broadcasted_iota(jnp.int32, (width, LANES), 1)
        swapped = pltpu.roll(columns, LANES - depth // 2, 1)
        crossed = pltpu.roll(columns, depth // 2, 1)
        zero = jnp.zeros_like(columns)
        right[:width, :] = jnp.where(column_lane < depth, columns, zero).astype(jnp.bfloat16)
        right[width:, :] = jnp.where(
            column_lane < depth // 2, swapped, jnp.where(column_lane < depth, -crossed, zero)
        ).astype(jnp.bfloat16)

    pick(rows, pl.program_id(0) * tile, tile)
    product = lax.dot_general(
        picked[:tile, :].astype(jnp.bfloat16), right[...], (((1,), (1,)), ((), ())),
        preferred_element_type=jnp.float32,
    )
    out_ref[0] = product[:, :width]
    out_ref[1] = product[:, width:]


def block_row(sources, reach, everything, phase_tangent, row_support, col_support):
    chunks = phase_tangent.shape[0] // LANES
    rows, width = row_support.shape[0], col_support.shape[0] // sources
    tile = TILE
    return pl.pallas_call(
        functools.partial(block_kernel, sources, chunks, reach, tile, width),
        out_shape=jax.ShapeDtypeStruct((2, rows, width), jnp.float32),
        grid=(rows // tile,),
        in_specs=[pl.BlockSpec(memory_space=pltpu.HBM)] * 4,
        out_specs=pl.BlockSpec((2, tile, width), lambda i: (0, i, 0)),
        scratch_shapes=[
            pltpu.SMEM(row_support.shape, jnp.int32),
            pltpu.SMEM(col_support.shape, jnp.int32),
            pltpu.VMEM(everything.shape, jnp.bfloat16),
            pltpu.VMEM((chunks, LANES), jnp.float32),
            pltpu.VMEM((3, reach * sources, LANES), jnp.float32),
            pltpu.VMEM((2 * sources, LANES), jnp.float32),
            pltpu.VMEM((reach * LANES, LANES), jnp.float32),
            pltpu.VMEM((max(tile, width), LANES), jnp.float32),
            pltpu.VMEM((2 * width, LANES), jnp.bfloat16),
            pltpu.SemaphoreType.DMA((4,)),
        ],
        name="block_row",
    )(row_support, col_support, everything, phase_tangent.reshape(chunks, LANES))


def local(n, pupils, phase_tangent, weights, weight_tangent, offsets, row_support, col_support):
    grid_size = phase_tangent.shape[0]
    rows = row_support.shape[0]
    width = col_support.shape[0] // n
    reach = grid_size // 6 * 5 // LANES
    fits = (
        PARTS * n == LANES
        and grid_size % (6 * LANES) == 0
        and rows % TILE == 0
        and width % LANES == 0
        and grid_size * LANES * 4 <= TABLE_LIMIT_BYTES
    )
    if not fits:
        return exchanged(pupils, phase_tangent, weights, weight_tangent, offsets, row_support, col_support)
    everything = gathered_pupils(n, reach, pupils, weights, weight_tangent, offsets)
    return block_row(n, reach, everything, phase_tangent, row_support, col_support)


def solution(mesh):
    in_specs = (
        P(None, ("groups", "col"), None),
        P(),
        P(("groups", "col")),
        P(("groups", "col")),
        P(("groups", "col")),
        P("groups"),
        P(),
    )
    out_specs = P(None, "groups", "col")
    return jax.shard_map(
        functools.partial(local, mesh.shape["col"]),
        mesh=mesh, in_specs=in_specs, out_specs=out_specs, check_vma=False,
    )
```

```python
import functools

import jax
import jax.numpy as jnp
from jax import lax
from jax.experimental import pallas as pl
from jax.experimental.pallas import tpu as pltpu
from jax.sharding import PartitionSpec as P

LANES = 128
PARTS = 8
PICKS = 256
TILE = 1024
ORDER = (1, 7, 2, 6, 3, 5, 4)
TABLE_LIMIT_BYTES = 8 * 1024 * 1024
MESH = pl.DeviceIdType.MESH


def shifted_values(pupils, offsets, support, phase_tangent):
    shifted = support[None, :] + offsets[:, None]
    real_part = jnp.take_along_axis(pupils[0], shifted, axis=1)
    imag_part = jnp.take_along_axis(pupils[1], shifted, axis=1)
    slopes = phase_tangent[shifted]
    return (real_part, imag_part, slopes)


def column_factors(real_part, imag_part, slopes, weights, weight_tangent):
    real_f = real_part.astype(jnp.float32)
    imag_f = imag_part.astype(jnp.float32)
    tangent_col = weight_tangent[:, None]
    weight_col = weights[:, None]
    x_real = (tangent_col * real_f - weight_col * slopes * imag_f).astype(jnp.bfloat16)
    x_imag = (tangent_col * imag_f + weight_col * slopes * real_f).astype(jnp.bfloat16)
    y_real = (weight_col * real_f).astype(jnp.bfloat16)
    y_imag = (weight_col * imag_f).astype(jnp.bfloat16)
    return jnp.stack([jnp.stack([x_real, y_real]), jnp.stack([x_imag, y_imag])])


def block_product(left_rows, col_block):
    width = col_block.shape[3]
    depth = 4 * col_block.shape[2]
    left_all = left_rows.reshape(depth, left_rows.shape[3])
    right_for_real = jnp.concatenate([col_block[0], col_block[1]], axis=0)
    right_for_imag = jnp.concatenate([col_block[1], -col_block[0]], axis=0)
    right_all = jnp.concatenate([right_for_real, right_for_imag], axis=2).reshape(depth, 2 * width)
    product = lax.dot_general(
        left_all, right_all, (((0,), (0,)), ((), ())), preferred_element_type=jnp.float32
    )
    return jnp.stack([product[:, :width], product[:, width:]])


def exchanged(pupils, phase_tangent, weights, weight_tangent, offsets, row_support, col_support):
    col_real, col_imag, col_slopes = shifted_values(pupils, offsets, col_support, phase_tangent)
    columns = column_factors(col_real, col_imag, col_slopes, weights, weight_tangent)
    col_block = lax.all_to_all(columns, "col", split_axis=3, concat_axis=2, tiled=True)
    row_real, row_imag, row_slopes = shifted_values(pupils, offsets, row_support, phase_tangent)
    d_real = (-row_slopes * row_imag.astype(jnp.float32)).astype(jnp.bfloat16)
    d_imag = (row_slopes * row_real.astype(jnp.float32)).astype(jnp.bfloat16)
    rows = jnp.stack([jnp.stack([row_real, d_real]), jnp.stack([row_imag, d_imag])])
    left_rows = lax.all_gather(rows, "col", axis=2, tiled=True)
    return block_product(left_rows, col_block)


def split3(value):
    high = value.astype(jnp.bfloat16).astype(jnp.float32)
    rest = value - high
    middle = rest.astype(jnp.bfloat16).astype(jnp.float32)
    return high, middle, rest - middle


def half_rows(reach):
    return (reach + 16) // 16 * 16


def shift_rows(source, start, reach, lane_shift, lane):
    lower = source[pl.ds(start, reach), :]
    upper = source[pl.ds(start + 1, reach), :]
    return pltpu.roll(jnp.where(lane >= lane_shift, lower, upper), (LANES - lane_shift) & (LANES - 1), 1)


def gather_kernel(
    n, chunks, reach, pupil_hbm, w_ref, wt_ref, off_ref, out_ref,
    pupil, wide, lined, packed, send_sem, recv_sem, own_sem,
):
    load = pltpu.make_async_copy(pupil_hbm, pupil, own_sem)
    load.start()
    me = lax.axis_index("col")
    sibling = me + 1 - 2 * lax.rem(me, 2)
    chips = n // 2

    def ahead(k):
        return lax.rem(me + 2 * k, n)

    barrier = pltpu.get_barrier_semaphore()
    for partner in [ahead(k) for k in range(1, chips)] + [sibling]:
        pl.semaphore_signal(barrier, inc=1, device_id={"col": partner}, device_id_type=MESH)

    half = half_rows(reach)
    scalar_rows = half - reach
    lane = lax.broadcasted_iota(jnp.int32, (scalar_rows, LANES), 1)
    scalars = jnp.zeros((scalar_rows, LANES), jnp.float32)
    place = 0
    for scalar in (w_ref[0], wt_ref[0], off_ref[0].astype(jnp.float32)):
        for piece in split3(jnp.full((scalar_rows, LANES), scalar, jnp.float32)):
            scalars = jnp.where(lane == place, piece, scalars)
            place += 1
    lined[reach:half, :] = scalars
    lined[half + reach :, :] = scalars
    start = lax.shift_right_logical(off_ref[0], LANES.bit_length() - 1)
    lane_shift = off_ref[0] & (LANES - 1)
    lane = lax.broadcasted_iota(jnp.int32, (reach, LANES), 1)
    load.wait()
    values = pupil[...].astype(jnp.float32)
    for part in range(2):
        for chunk in range(chunks):
            row = part * chunks + chunk
            wide[row : row + 1, :] = values[part : part + 1, chunk * LANES : (chunk + 1) * LANES]
    lined[:reach, :] = shift_rows(wide, start, reach, lane_shift, lane)
    lined[half : half + reach, :] = shift_rows(wide, chunks + start, reach, lane_shift, lane)
    packed[...] = lined[...].astype(jnp.bfloat16)

    own = pltpu.make_async_copy(packed, out_ref.at[me], own_sem)
    own.start()
    pl.semaphore_wait(barrier, chips)

    def send(source, slot, index, partner):
        copy = pltpu.make_async_remote_copy(
            src_ref=source,
            dst_ref=out_ref.at[slot],
            send_sem=send_sem.at[index],
            recv_sem=recv_sem.at[index],
            device_id={"col": partner},
            device_id_type=MESH,
        )
        copy.start()
        return copy

    copies = {k: send(packed, me, k, ahead(k)) for k in range(1, chips)}
    copies[chips] = send(packed, me, chips, sibling)
    for k in ORDER:
        copies[k].wait_recv()
        slot = ahead(chips - k)
        copies[chips + k] = send(out_ref.at[slot], slot, chips + k, sibling)
    own.wait()
    for k in range(chips):
        copies[chips + k].wait_recv()
    for k in range(1, n):
        copies[k].wait_send()


def gathered_pupils(n, reach, pupils, weights, weight_tangent, offsets):
    grid_size = pupils.shape[2]
    chunks = grid_size // LANES
    rows = 2 * half_rows(reach)
    smem = pl.BlockSpec(memory_space=pltpu.SMEM)
    return pl.pallas_call(
        functools.partial(gather_kernel, n, chunks, reach),
        out_shape=jax.ShapeDtypeStruct((n, rows, LANES), jnp.bfloat16),
        in_specs=[pl.BlockSpec(memory_space=pltpu.HBM), smem, smem, smem],
        out_specs=pl.BlockSpec(memory_space=pltpu.HBM),
        scratch_shapes=[
            pltpu.VMEM((2, grid_size), jnp.bfloat16),
            pltpu.VMEM((2 * chunks, LANES), jnp.float32),
            pltpu.VMEM((rows, LANES), jnp.float32),
            pltpu.VMEM((rows, LANES), jnp.bfloat16),
            pltpu.SemaphoreType.DMA((n,)),
            pltpu.SemaphoreType.DMA((n,)),
            pltpu.SemaphoreType.DMA,
        ],
        compiler_params=pltpu.CompilerParams(collective_id=0, has_side_effects=True),
        name="gather_pupils",
    )(pupils.reshape(2, grid_size), weights, weight_tangent, offsets)


def block_kernel(
    sources, chunks, reach, tile, width,
    row_hbm, col_hbm, all_hbm, phase_hbm, out_ref,
    rows, cols, everything, phase, shifted, factors, table, picked, right, sems,
):
    depth = 4 * sources

    def pick(index_ref, base, count):
        def some(group, carry):
            first = pl.multiple_of(group * PICKS, 8)
            for k in range(PICKS):
                picked[pl.ds(first + k, 1), :] = table[pl.ds(index_ref[base + first + k], 1), :]
            return carry

        lax.fori_loop(0, count // PICKS, some, 0)

    @pl.when(pl.program_id(0) == 0)
    def _():
        copies = [
            pltpu.make_async_copy(source, target, sems.at[i])
            for i, (source, target) in enumerate(
                [(all_hbm, everything), (phase_hbm, phase), (row_hbm, rows), (col_hbm, cols)]
            )
        ]
        for copy in copies:
            copy.start()
        copies[0].wait()
        copies[1].wait()
        lane = lax.broadcasted_iota(jnp.int32, (reach, LANES), 1)
        half = half_rows(reach)
        for s in range(sources):
            spread = pl.ds(s, reach, stride=sources)
            real = everything[s, :half, :].astype(jnp.float32)
            shifted[0, spread, :] = real[:reach, :]
            shifted[1, spread, :] = everything[s, half:, :].astype(jnp.float32)[:reach, :]
            scalars = real[reach : reach + 1, :]
            one, two, three = (
                scalars[:, i : i + 1] + scalars[:, i + 1 : i + 2] + scalars[:, i + 2 : i + 3] for i in (0, 3, 6)
            )
            factors[s : s + 1, :] = jnp.broadcast_to(one, (1, LANES))
            factors[sources + s : sources + s + 1, :] = jnp.broadcast_to(two, (1, LANES))
            offset = three[0, 0].astype(jnp.int32)
            start = lax.shift_right_logical(offset, LANES.bit_length() - 1)
            shifted[2, spread, :] = shift_rows(phase, start, reach, offset & (LANES - 1), lane)
        weight = factors[:sources, :]
        tangent = factors[sources:, :]

        def one_chunk(chunk, carry):
            at = pl.ds(pl.multiple_of(chunk * sources, sources), sources)
            real, imag, slope = shifted[0, at, :], shifted[1, at, :], shifted[2, at, :]
            tilted = weight * slope
            block = jnp.concatenate(
                [
                    real,
                    -slope * imag,
                    imag,
                    slope * real,
                    tangent * real - tilted * imag,
                    weight * real,
                    tangent * imag + tilted * real,
                    weight * imag,
                ],
                axis=0,
            )
            table[pl.ds(pl.multiple_of(chunk * LANES, LANES), LANES), :] = block.astype(jnp.bfloat16).T.astype(jnp.float32)
            return carry

        lax.fori_loop(0, reach, one_chunk, 0, unroll=20)

        copies[2].wait()
        copies[3].wait()
        pick(cols, lax.axis_index("col") * width, width)
        columns = pltpu.roll(picked[:width, :], PARTS * sources - depth, 1)
        column_lane = lax.broadcasted_iota(jnp.int32, (width, LANES), 1)
        swapped = pltpu.roll(columns, LANES - depth // 2, 1)
        crossed = pltpu.roll(columns, depth // 2, 1)
        zero = jnp.zeros_like(columns)
        right[:width, :] = jnp.where(column_lane < depth, columns, zero).astype(jnp.bfloat16)
        right[width:, :] = jnp.where(
            column_lane < depth // 2, swapped, jnp.where(column_lane < depth, -crossed, zero)
        ).astype(jnp.bfloat16)

    pick(rows, pl.program_id(0) * tile, tile)
    product = lax.dot_general(
        picked[:tile, :].astype(jnp.bfloat16), right[...], (((1,), (1,)), ((), ())),
        preferred_element_type=jnp.float32,
    )
    out_ref[0] = product[:, :width]
    out_ref[1] = product[:, width:]


def block_row(sources, reach, everything, phase_tangent, row_support, col_support):
    chunks = phase_tangent.shape[0] // LANES
    rows, width = row_support.shape[0], col_support.shape[0] // sources
    tile = TILE
    return pl.pallas_call(
        functools.partial(block_kernel, sources, chunks, reach, tile, width),
        out_shape=jax.ShapeDtypeStruct((2, rows, width), jnp.float32),
        grid=(rows // tile,),
        in_specs=[pl.BlockSpec(memory_space=pltpu.HBM)] * 4,
        out_specs=pl.BlockSpec((2, tile, width), lambda i: (0, i, 0)),
        scratch_shapes=[
            pltpu.SMEM(row_support.shape, jnp.int32),
            pltpu.SMEM(col_support.shape, jnp.int32),
            pltpu.VMEM(everything.shape, jnp.bfloat16),
            pltpu.VMEM((chunks, LANES), jnp.float32),
            pltpu.VMEM((3, reach * sources, LANES), jnp.float32),
            pltpu.VMEM((2 * sources, LANES), jnp.float32),
            pltpu.VMEM((reach * LANES, LANES), jnp.float32),
            pltpu.VMEM((max(tile, width), LANES), jnp.float32),
            pltpu.VMEM((2 * width, LANES), jnp.bfloat16),
            pltpu.SemaphoreType.DMA((4,)),
        ],
        name="block_row",
    )(row_support, col_support, everything, phase_tangent.reshape(chunks, LANES))


def local(n, pupils, phase_tangent, weights, weight_tangent, offsets, row_support, col_support):
    grid_size = phase_tangent.shape[0]
    rows = row_support.shape[0]
    width = col_support.shape[0] // n
    reach = grid_size // 6 * 5 // LANES
    fits = (
        PARTS * n == LANES
        and grid_size % (6 * LANES) == 0
        and rows % TILE == 0
        and width % LANES == 0
        and grid_size * LANES * 4 <= TABLE_LIMIT_BYTES
    )
    if not fits:
        return exchanged(pupils, phase_tangent, weights, weight_tangent, offsets, row_support, col_support)
    everything = gathered_pupils(n, reach, pupils, weights, weight_tangent, offsets)
    return block_row(n, reach, everything, phase_tangent, row_support, col_support)


def solution(mesh):
    in_specs = (
        P(None, ("groups", "col"), None),
        P(),
        P(("groups", "col")),
        P(("groups", "col")),
        P(("groups", "col")),
        P("groups"),
        P(),
    )
    out_specs = P(None, "groups", "col")
    return jax.shard_map(
        functools.partial(local, mesh.shape["col"]),
        mesh=mesh, in_specs=in_specs, out_specs=out_specs, check_vma=False,
    )
```
